32 devices in a mesh: ao: 4 (over y, x), prow: 4 (over z), pcol: 2 (over core).
Axes of the slice: x: 2, y: 2, z: 4, core: 2. Of those that a mesh axis runs over, the one named last changes fastest.
Arguments:
- three_index: bfloat16 [512, 1200, 1200], P(('prow', 'pcol'), 'ao'), may hold values from -1.2578125 to 1.2578125
- coefficients: bfloat16 [1200, 120], replicated, may hold values from -0.1875 to 0.1875
Outputs:
- coulomb: bfloat16 [14400, 14400], P('ao', ('prow', 'pcol'))
The draws below stay inside these ranges and needn't reach their ends.
All inputs are finite; a program needn't handle non-finite values.
Results may differ from the reference program's by a relative error of at most 0.0069.
Values may be sent and summed in bfloat16 or wider, within the bound.
A program may use at most 256 MiB of HBM per device.

```python
import jax
import jax.numpy as jnp
from jax import lax

N = 1200
A = 120
AUX_DEV = 64
AUX = 512


def block_scale(stream_key, extent, cuts, least, largest):
    gain, own = 1.0, jax.random.fold_in(stream_key, 6)
    for axis_at, blocks in cuts:
        heights = jnp.exp(jax.random.uniform(jax.random.fold_in(own, axis_at), (blocks,), jnp.float32, least / len(cuts), largest / len(cuts)))
        gain = gain * jnp.repeat(heights, extent[axis_at] // blocks).reshape([-1 if axis == axis_at else 1 for axis in range(len(extent))])
    return gain


def centred(key, extent, width, limit, cuts=(), dtype=jnp.bfloat16):
    drawn = jax.random.normal(key, extent, jnp.float32) * width
    if len(cuts) > 0:
        drawn = block_scale(key, extent, cuts, -0.22, 0.18) * drawn
    return jnp.clip(drawn, min=-limit, max=limit).astype(dtype)


def setup_inputs(seed: int = 0) -> dict:
    keys = jax.random.split(jax.random.key(seed), 3)
    return {
        "three_index": centred(keys[0], (AUX, N, N), (AUX ** -0.25), 1.2578125, ((0, 8), (1, 4))),
        "coefficients": centred(keys[1], (N, A), N ** -0.5, 0.1875),
    }


def reference(three_index, coefficients):
    def transform(block):
        half = jnp.dot(block.reshape(-1, N), coefficients, preferred_element_type=jnp.float32)
        half = half.astype(jnp.bfloat16).reshape(-1, N, A)
        summed = jnp.einsum("mp,amq->apq", coefficients.astype(jnp.float32), half.astype(jnp.float32))
        return summed.reshape(-1, A * A).astype(jnp.bfloat16)

    blocks = three_index.reshape(AUX // AUX_DEV, AUX_DEV, N, N)
    pair_ints = lax.map(transform, blocks).reshape(AUX, A * A)
    coulomb = lax.dot_general(pair_ints, pair_ints, (((0,), (0,)), ((), ())), preferred_element_type=jnp.float32)
    return coulomb.astype(jnp.bfloat16)
```

```python
import functools

import jax
import jax.numpy as jnp
from jax import lax
from jax.experimental import pallas as pl
from jax.experimental.pallas import tpu as pltpu
from jax.sharding import PartitionSpec as P

CHUNK = 16
SLOTS = 4
MESH = pl.DeviceIdType.MESH


def rounded(size, unit):
    return -(-size // unit) * unit


def kernel(
    dims, three_ref, coef_ref, rows_ref, x_out, y_out,
    ring, halves, part, sending, arrived, own, pack, x, y,
    ring_sem, rs_send, rs_recv, ag_send, ag_recv, sib_send, sib_recv, y_send, y_recv, out_sem,
):
    nao, nrow, ncol, chunks, active, width, panels = dims
    ao, row, col = lax.axis_index("ao"), lax.axis_index("prow"), lax.axis_index("pcol")
    groups = nrow * ncol
    block = active // nao
    block_rows = block * CHUNK
    batch = ring.shape[1]
    basis_rows = three_ref.shape[0]
    steps = basis_rows // batch
    total_steps = chunks * steps

    def load(step, slot):
        return pltpu.make_async_copy(
            three_ref.at[
                pl.ds(lax.rem(step, steps) * batch, batch),
                pl.ds(pl.multiple_of(lax.div(step, steps) * CHUNK, CHUNK), CHUNK),
            ],
            ring.at[slot],
            ring_sem.at[slot],
        )

    for slot in range(SLOTS):
        load(slot, slot).start()

    barrier = pltpu.get_barrier_semaphore()
    partners = [{"ao": lax.rem(ao + d, nao)} for d in range(1, nao)]
    partners += [{"pcol": lax.rem(col + d, ncol)} for d in range(1, ncol)]
    partners += [{"prow": lax.rem(row + d, nrow)} for d in range(1, nrow)]
    for partner in partners:
        pl.semaphore_signal(barrier, inc=1, device_id=partner, device_id_type=MESH)
    pl.semaphore_wait(barrier, len(partners))

    pack[...] = jnp.zeros_like(pack)

    def remote(src, dst, send, recv, where):
        return pltpu.make_async_remote_copy(
            src_ref=src, dst_ref=dst, send_sem=send, recv_sem=recv,
            device_id=where, device_id_type=MESH,
        )

    def panel_rows(j, at_row, at_col):
        start = (j * groups + at_row * ncol + at_col) * CHUNK
        return pl.ds(pl.multiple_of(start, CHUNK), CHUNK)

    def pair_rows(j, at_row):
        start = (j * groups + at_row * ncol) * CHUNK
        return pl.ds(pl.multiple_of(start, CHUNK), ncol * CHUNK)

    def rs_copy(j, d):
        target = lax.rem(ao + d, nao)
        src = sending.at[j, pl.ds(pl.multiple_of(target * block_rows, CHUNK), block_rows)]
        return remote(
            src, arrived.at[j, d - 1], rs_send.at[j, d - 1], rs_recv.at[j, d - 1], {"ao": target}
        )

    def ag_copy(j, origin, hop, direction):
        at = x.at[panel_rows(j, origin, col)]
        where = {"prow": row + 1 if direction == 0 else row - 1}
        return remote(at, at, ag_send.at[j, hop, direction], ag_recv.at[j, hop, direction], where)

    def sib_copy(j, origin, slot, d):
        at = x.at[panel_rows(j, origin, col)]
        where = {"pcol": lax.rem(col + d, ncol)}
        return remote(at, at, sib_send.at[j, slot, d - 1], sib_recv.at[j, slot, d - 1], where)

    def sib_arrival(j, origin, slot, d):
        source = lax.rem(col + ncol - d, ncol)
        at = x.at[panel_rows(j, origin, source)]
        where = {"pcol": lax.rem(col + d, ncol)}
        return remote(at, at, sib_send.at[j, slot, d - 1], sib_recv.at[j, slot, d - 1], where)

    def ring_place(index):
        half = lax.div(index, 2)
        return jnp.where(lax.rem(index, 2) == 0, half, nao - 1 - half)

    def ring_index(place):
        return jnp.where(place < nao // 2, 2 * place, 2 * (nao - 1 - place) + 1)

    place, owner = ring_place(ao), ring_place(row)
    away = (lax.rem(place - owner + nao, nao), lax.rem(owner - place + nao, nao))
    onward = (
        ring_index(lax.rem(place + 1, nao)),
        ring_index(lax.rem(place + nao - 1, nao)),
    )

    def y_copy(j, origin, slot, way):
        at = y.at[pair_rows(j, origin)]
        return remote(at, at, y_send.at[j, slot], y_recv.at[j, slot], {"ao": onward[way]})

    def cut(j, origin):
        rows = pair_rows(j, origin)
        for h in range(panels):
            @pl.when(col == h)
            def _():
                low = h * width
                base = low // 128 * 128
                stop = rounded(low + width, 128)
                wide = x[rows, base:stop].astype(jnp.float32)
                piece = wide[:, low - base:low - base + width]
                y[rows, :width] = piece.astype(jnp.bfloat16)

    places = [(0, 0, 0, row, row >= 0)]
    for hop in range(1, nrow):
        places.append((2 * hop - 1, hop, 0, row - hop, row - hop >= 0))
        places.append((2 * hop, hop, 1, row + hop, row + hop < nrow))

    def compute(j):
        def body(i, carry):
            step = j * steps + i
            slot = lax.rem(step, SLOTS)
            load(step, slot).wait()
            rows = ring[slot].reshape(batch * CHUNK, ring.shape[3])
            start = pl.multiple_of(i * (batch * CHUNK), CHUNK)
            halves[pl.ds(start, batch * CHUNK), :] = jnp.dot(
                rows, coef_ref[...], preferred_element_type=jnp.float32
            )

            @pl.when(step + SLOTS < total_steps)
            def _():
                load(step + SLOTS, slot).start()

            return carry

        lax.fori_loop(0, steps, body, 0)
        for u in range(CHUNK):
            half = halves[pl.ds(u, basis_rows, stride=CHUNK), :].astype(jnp.bfloat16)
            part[pl.ds(u, active, stride=CHUNK), :] = jnp.dot(
                rows_ref[...], half, preferred_element_type=jnp.float32
            )
        sending[j] = part[...].astype(jnp.bfloat16)
        own[j] = part[pl.ds(pl.multiple_of(ao * block_rows, CHUNK), block_rows), :]
        for d in range(1, nao):
            rs_copy(j, d).start()

    def combine(j):
        for d in range(1, nao):
            rs_copy(j, d).wait_recv()
        for p in range(block):
            rows = pl.ds(p * CHUNK, CHUNK)
            value = own[j, rows, :]
            for d in range(1, nao):
                value = value + arrived[j, d - 1, rows, :].astype(jnp.float32)
            first = p * active
            pack[:, first:first + active] = value[:, :active]
        x[panel_rows(j, row, col), :] = pack[...].astype(jnp.bfloat16)

        @pl.when(row < nrow - 1)
        def _():
            ag_copy(j, row, 1, 0).start()

        @pl.when(row > 0)
        def _():
            ag_copy(j, row, 1, 1).start()

        for d in range(1, ncol):
            sib_copy(j, row, 0, d).start()

    def onward_on_line(direction):
        return row < nrow - 1 if direction == 0 else row > 0

    def in_chunks(j):
        return jnp.logical_and(j >= 0, j < chunks)

    def tick(t, carry):
        @pl.when(t < chunks)
        def _():
            compute(t)

        @pl.when(in_chunks(t - 1))
        def _():
            combine(t - 1)

        for slot, hop, direction, origin, there in places:
            if hop == 0:
                continue
            j = t - 1 - hop

            @pl.when(jnp.logical_and(in_chunks(j), there))
            def _():
                ag_copy(j, origin, hop, direction).wait_recv()
                if hop < nrow - 1:
                    @pl.when(onward_on_line(direction))
                    def _():
                        ag_copy(j, origin, hop + 1, direction).start()
                for d in range(1, ncol):
                    sib_copy(j, origin, slot, d).start()

        for slot, hop, direction, origin, there in places:
            j = t - 2 - hop

            @pl.when(jnp.logical_and(in_chunks(j), there))
            def _():
                for d in range(1, ncol):
                    sib_arrival(j, origin, slot, d).wait_recv()

            for way in range(2):
                k = t - 2 - hop - away[way]
                mine = lax.rem(k + slot + 2 * chunks * nrow * nao, 2) == way

                @pl.when(jnp.logical_and(jnp.logical_and(in_chunks(k), there), mine))
                def _():
                    @pl.when(away[way] == 0)
                    def _():
                        cut(k, origin)
                        y_copy(k, origin, slot, way).start()

                    @pl.when(away[way] > 0)
                    def _():
                        y_copy(k, origin, slot, way).wait_recv()

                        @pl.when(away[way] < nao - 1)
                        def _():
                            y_copy(k, origin, slot, way).start()

        return carry

    lax.fori_loop(0, chunks + nrow + nao, tick, 0)

    x_copy = pltpu.make_async_copy(x, x_out, out_sem.at[0])
    x_copy.start()

    y_finish = pltpu.make_async_copy(y, y_out, out_sem.at[1])
    y_finish.start()
    y_finish.wait()
    x_copy.wait()

    def drain(j, carry):
        for d in range(1, nao):
            rs_copy(j, d).wait_send()
        for slot, hop, direction, origin, there in places:
            @pl.when(there)
            def _():
                for d in range(1, ncol):
                    sib_copy(j, origin, slot, d).wait_send()
                if hop < nrow - 1:
                    for way in ((0, 1) if hop == 0 else (direction,)):
                        @pl.when(onward_on_line(way))
                        def _():
                            ag_copy(j, origin, hop + 1, way).wait_send()
                for way in range(2):
                    mine = lax.rem(j + slot, 2) == way

                    @pl.when(jnp.logical_and(mine, away[way] < nao - 1))
                    def _():
                        y_copy(j, origin, slot, way).wait_send()

        return carry

    lax.fori_loop(0, chunks, drain, 0)


def on_device(sizes, three_index, coefficients):
    nao, nrow, ncol = sizes
    aux_local, rows_local, basis = three_index.shape
    active = coefficients.shape[1]
    pairs = active * active
    groups = nrow * ncol
    assert nao == nrow and groups % nao == 0 and groups // nao == ncol
    assert active % nao == 0 and aux_local % CHUNK == 0
    panels = ncol
    width = pairs // groups
    padded = rounded(width, 128)
    row_width = pairs // nao
    row_padded = rounded(row_width, 128)
    steps = max(s for s in range(1, 6) if rows_local % s == 0)
    lanes = rounded(active, 128)
    chunks = aux_local // CHUNK
    aux = aux_local * groups
    block_rows = active // nao * CHUNK
    local_rows = lax.dynamic_slice_in_dim(
        coefficients, lax.axis_index("ao") * rows_local, rows_local, 0
    ).T
    coefs = jnp.pad(coefficients, ((0, 0), (0, lanes - active)))
    dma = pltpu.SemaphoreType.DMA
    dims = (nao, nrow, ncol, chunks, active, width, panels)
    x, y = pl.pallas_call(
        functools.partial(kernel, dims),
        out_shape=(
            jax.ShapeDtypeStruct((aux, row_padded), jnp.bfloat16),
            jax.ShapeDtypeStruct((aux, padded), jnp.bfloat16),
        ),
        in_specs=[
            pl.BlockSpec(memory_space=pl.ANY),
            pl.BlockSpec(memory_space=pltpu.VMEM),
            pl.BlockSpec(memory_space=pltpu.VMEM),
        ],
        out_specs=(pl.BlockSpec(memory_space=pl.ANY), pl.BlockSpec(memory_space=pl.ANY)),
        scratch_shapes=[
            pltpu.VMEM((SLOTS, rows_local // steps, CHUNK, basis), jnp.bfloat16),
            pltpu.VMEM((rows_local * CHUNK, lanes), jnp.float32),
            pltpu.VMEM((active * CHUNK, lanes), jnp.float32),
            pltpu.VMEM((chunks, active * CHUNK, lanes), jnp.bfloat16),
            pltpu.VMEM((chunks, nao - 1, block_rows, lanes), jnp.bfloat16),
            pltpu.VMEM((chunks, block_rows, lanes), jnp.float32),
            pltpu.VMEM((CHUNK, row_padded), jnp.float32),
            pltpu.VMEM((aux, row_padded), jnp.bfloat16),
            pltpu.VMEM((aux, padded), jnp.bfloat16),
            dma((SLOTS,)),
            dma((chunks, nao - 1)),
            dma((chunks, nao - 1)),
            dma((chunks, nrow, 2)),
            dma((chunks, nrow, 2)),
            dma((chunks, 2 * nrow - 1, ncol - 1)),
            dma((chunks, 2 * nrow - 1, ncol - 1)),
            dma((chunks, 2 * nrow - 1)),
            dma((chunks, 2 * nrow - 1)),
            dma((2,)),
        ],
        compiler_params=pltpu.CompilerParams(
            collective_id=0, has_side_effects=True, vmem_limit_bytes=44 * 2**20
        ),
    )(jnp.transpose(three_index, (1, 0, 2)), coefs, local_rows)
    mirrored = lax.dot_general(
        y[:, :width], x[:, :row_width], (((0,), (0,)), ((), ())), preferred_element_type=jnp.float32
    )
    return mirrored.astype(jnp.bfloat16).T


def solution(mesh):
    sizes = tuple(mesh.shape[axis] for axis in ("ao", "prow", "pcol"))
    placed = (P(("prow", "pcol"), "ao", None), P())
    return jax.shard_map(
        functools.partial(on_device, sizes), mesh=mesh, in_specs=placed,
        out_specs=P("ao", ("prow", "pcol")), check_vma=False,
    )
```
